512 devices in a mesh: occ: 16 (over y, core), vir: 32 (over x, z).
Axes of the slice: x: 4, y: 8, z: 8, core: 2. Of those that a mesh axis runs over, the one named last changes fastest.
Arguments:
- amplitudes: float32 [2048, 12288], P('occ', 'vir'), may hold values from -6 to 6
- integrals: float32 [12288, 4096], P('vir', 'occ'), may hold values from -0.109375 to 0.109375
- pair_mask: int32 [32, 192], P('occ', 'vir'), may hold values 0 or 1
- tile_mask: int32 [192, 64], P('vir', 'occ'), may hold values 0 or 1
Outputs:
- residual: float32 [2048, 4096], P('occ', 'vir')
The draws below stay inside these ranges and needn't reach their ends.
Inputs may be any that keep to these rules, and one draw needn't show every extreme that they name: `pair_mask`: 0 marks a tile that is absent and contributes nothing. `tile_mask`: 0 marks a tile that is absent and contributes nothing.
All inputs are finite; a program needn't handle non-finite values. No bound on the sum of `pair_mask` or of `tile_mask` on one device may be relied on, other than what follows from the above.
Results may differ from the reference program's by a relative error of at most 0.00007.
Values sent between devices are 32-bit elements; how exact they have to be, the bound alone decides.
No kernel may reach another device: no remote copies, remote signals or barrier semaphores. Data moves between devices by JAX's collectives and lax.ppermute only.
A program may use at most 64 MiB of HBM per device.

```python
import jax
import jax.numpy as jnp
from jax import lax

TILE = 64
PAIRS = 2048
CD_TILES = 192
AB_TILES = 64


def set_ends(result, own_key, low, top_value):
    longest = result.shape.index(max(result.shape))
    spots = []
    for shift in (0, 1):
        where = [jax.random.randint(jax.random.fold_in(own_key, axis), (), 0, length) for axis, length in enumerate(result.shape)]
        where[longest] = (where[longest] + shift) % result.shape[longest]
        spots.append(tuple(where))
    return result.at[spots[0]].set(low).at[spots[1]].set(top_value)


def raised(array, rng, source, target, shards_of, factor):
    owner, partner = [(jnp.arange(array.shape[axis_at]) // (array.shape[axis_at] // shards_of)).reshape([-1 if axis == axis_at else 1 for axis in range(array.ndim)]) for axis_at in (source, target)]
    chosen = jax.random.permutation(rng, shards_of)[partner]
    strong = (owner == chosen) | (owner == (partner + shards_of // 2) % shards_of)
    return jnp.where(strong, factor * array, array)


def shard_levels(rng, dims, pieces, smallest, high):
    def one(position, parts):
        steps = jax.random.uniform(jax.random.fold_in(jax.random.fold_in(rng, 6), position), (parts,), jnp.float32, smallest / len(pieces), high / len(pieces))
        return jnp.repeat(jnp.exp(steps), dims[position] // parts).reshape((-1,) + (1,) * (len(dims) - position - 1))

    gain = one(*pieces[0])
    for cut in pieces[1:]:
        gain = gain * one(*cut)
    return gain


def centred(own_key, extent, spread, most, cuts=(), kind=jnp.bfloat16):
    result = jax.random.normal(own_key, extent, jnp.float32) * spread
    if len(cuts) > 0:
        result = shard_levels(own_key, extent, cuts, -0.22, 0.18) * result
    return jnp.clip(result, min=-most, max=most).astype(kind)


def bell_draw_with(key, dims, scale, bound, shards, heavy, kind=jnp.bfloat16):
    array = scale * jax.random.normal(key, dims, jnp.float32)
    if shards:
        array = array * shard_levels(key, dims, shards, -0.22, 0.18)
    return jnp.clip(raised(array, jax.random.fold_in(key, 3), *heavy), -bound, bound).astype(kind)


def setup_inputs(seed: int = 0) -> dict:
    key_list = jax.random.split(jax.random.key(seed), 5)
    return {
        "amplitudes": centred(key_list[0], (PAIRS, CD_TILES * TILE), 1.0, 6.0, ((0, 16), (1, 32)), jnp.float32),
        "integrals": bell_draw_with(key_list[1], (CD_TILES * TILE, AB_TILES * TILE), (CD_TILES * TILE) ** -0.5, 0.109375, ((0, 32), (1, 16)), (0, 1, 32, 2.75), jnp.float32),
        "pair_mask": set_ends((jax.random.randint(key_list[2], (PAIRS // TILE, CD_TILES), 0, 3) < 2).astype(jnp.int32), jax.random.fold_in(key_list[2], 1), 0, 1),
        "tile_mask": set_ends((jax.random.randint(key_list[3], (CD_TILES, AB_TILES), 0, 2) < 1).astype(jnp.int32), jax.random.fold_in(key_list[3], 1), 0, 1),
    }


def expand(mask, width):
    grown = jnp.repeat(mask.astype(jnp.float32), width, axis=0)
    return jnp.repeat(grown, width, axis=1)


def reference(amplitudes, integrals, pair_mask, tile_mask):
    masked_t = amplitudes * expand(pair_mask, TILE)
    masked_v = integrals * expand(tile_mask, TILE)
    return jnp.dot(masked_t, masked_v, precision=lax.Precision.HIGHEST, preferred_element_type=jnp.float32)
```

```python
import jax
import jax.numpy as jnp
from jax import lax
from jax.sharding import Mesh, PartitionSpec as P


def expand(mask, width):
    grown = jnp.repeat(mask.astype(jnp.float32), width, axis=0)
    return jnp.repeat(grown, width, axis=1)


def body(amplitudes, integrals, pair_mask, tile_mask):
    tile_width = amplitudes.shape[1] // pair_mask.shape[1]
    masked_v = integrals * expand(tile_mask, tile_width)
    other_v = lax.ppermute(masked_v, "l", [(0, 1), (1, 0)])
    masked_t = amplitudes * expand(pair_mask, tile_width)
    rows = lax.all_gather(masked_t, "h", axis=0, tiled=True)
    near = lax.all_gather(masked_v, "c", axis=1, tiled=True)
    far = lax.all_gather(other_v, "c", axis=1, tiled=True)
    low = lax.axis_index("l") == 0
    columns = jnp.concatenate([jnp.where(low, near, far), jnp.where(low, far, near)], axis=1)
    partial_sum = jnp.dot(rows, columns, precision=lax.Precision.HIGH, preferred_element_type=jnp.float32)
    count = lax.axis_size("x")
    parts = lax.all_to_all(partial_sum, "x", 0, 0, tiled=True)
    over_x = parts.reshape(count, -1, parts.shape[1]).sum(0)
    depth = lax.axis_size("z")
    pieces = over_x.reshape(over_x.shape[0], depth, -1).transpose(1, 0, 2)
    pieces = lax.all_to_all(pieces, "z", 0, 0, tiled=True)
    total = pieces.sum(0)
    swap = [(h * count + x, x * count + h) for h in range(count) for x in range(count)]
    return lax.ppermute(total, ("h", "x"), swap)


def solution(mesh):
    fine = Mesh(mesh.devices.reshape(4, 2, 2, 4, 8), ("h", "l", "c", "x", "z"))
    occ, vir = ("h", "l", "c"), ("x", "z")
    in_specs = (P(occ, vir), P(vir, occ), P(occ, vir), P(vir, occ))
    return jax.shard_map(body, mesh=fine, in_specs=in_specs, out_specs=P(occ, vir), check_vma=False)
```

```python
import jax
import jax.numpy as jnp
from jax import lax
from jax.sharding import Mesh, PartitionSpec as P

AXES = ("h", "l", "c", "x", "z")
SIZES = (4, 2, 2, 4, 8)


def moves(names, target):
    sizes = [SIZES[AXES.index(name)] for name in names]
    pairs = []
    total = 1
    for size in sizes:
        total *= size
    for source in range(total):
        rest, at = source, {}
        for name, size in zip(names[::-1], sizes[::-1]):
            at[name], rest = rest % size, rest // size
        to = dict(at, **target(at))
        index = 0
        for name, size in zip(names, sizes):
            index = index * size + to[name] % size
        pairs.append((source, index))
    return pairs


def send(value, names, target):
    return lax.ppermute(value, names, moves(names, target))


def expand(mask, width):
    grown = jnp.repeat(mask.astype(jnp.float32), width, axis=0)
    return jnp.repeat(grown, width, axis=1)


def product(a, b):
    return jnp.dot(a, b, precision=lax.Precision.HIGH, preferred_element_type=jnp.float32)


def sign(at):
    return 1 - 2 * ((at["x"] + at["c"]) % 2)


def body(amplitudes, integrals, pair_mask, tile_mask):
    l = lax.axis_index("l")
    width = amplitudes.shape[1] // pair_mask.shape[1]
    masked_v = integrals * expand(tile_mask, width)
    far_half = send(masked_v, ("l",), lambda at: {"l": at["l"] + 1})
    near = lax.all_gather(masked_v, "c", axis=1, tiled=True)
    near_beside = send(near, ("c", "x"), lambda at: {"x": at["x"] + sign(at)})
    masked_t = amplitudes * expand(pair_mask, width)
    names = ("h", "c", "x")
    own = jnp.concatenate([
        send(masked_t, names, lambda at: {"h": at["h"] - at["x"]}),
        send(masked_t, names, lambda at: {"h": at["h"] - at["x"] + sign(at)}),
    ])
    beside = jnp.concatenate([
        send(masked_t, names, lambda at: {"h": at["h"] - at["x"] - sign(at), "x": at["x"] + sign(at)}),
        send(masked_t, names, lambda at: {"h": at["h"] - at["x"] - 2 * sign(at), "x": at["x"] + sign(at)}),
    ])
    far = lax.all_gather(far_half, "c", axis=1, tiled=True)
    far_beside = send(far, ("c", "x"), lambda at: {"x": at["x"] + sign(at)})
    near_sum = product(own, near) + product(beside, near_beside)
    far_sum = product(own, far) + product(beside, far_beside)
    away = jnp.concatenate([near_sum[128:], far_sum[128:]], axis=1)
    came = send(away, ("c", "x"), lambda at: {"x": at["x"] - sign(at)})
    near_sum, far_sum = near_sum[:128] + came[:, :512], far_sum[:128] + came[:, 512:]
    low = l == 0
    halves = jnp.concatenate([jnp.where(low, near_sum, far_sum), jnp.where(low, far_sum, near_sum)], axis=1)
    pieces = halves.reshape(128, 8, 128).transpose(1, 0, 2)
    total = lax.all_to_all(pieces, "z", 0, 0, tiled=True).sum(0)
    return send(total, ("h", "x"), lambda at: {"h": at["h"] + at["x"], "x": at["h"]})


def solution(mesh):
    fine = Mesh(mesh.devices.reshape(SIZES), AXES)
    occ, vir = ("h", "l", "c"), ("x", "z")
    in_specs = (P(occ, vir), P(vir, occ), P(occ, vir), P(vir, occ))
    return jax.shard_map(body, mesh=fine, in_specs=in_specs, out_specs=P(occ, vir), check_vma=False)
```

```python
import jax
import jax.numpy as jnp
from jax import lax
from jax.sharding import Mesh, PartitionSpec as P

AXES = ("h", "l", "c", "x", "z")
SIZES = (4, 2, 2, 4, 8)


def moves(names, target):
    sizes = [SIZES[AXES.index(name)] for name in names]
    pairs = []
    total = 1
    for size in sizes:
        total *= size
    for source in range(total):
        rest, at = source, {}
        for name, size in zip(names[::-1], sizes[::-1]):
            at[name], rest = rest % size, rest // size
        to = dict(at, **target(at))
        index = 0
        for name, size in zip(names, sizes):
            index = index * size + to[name] % size
        pairs.append((source, index))
    return pairs


def send(value, names, target):
    return lax.ppermute(value, names, moves(names, target))


def expand(mask, width):
    grown = jnp.repeat(mask.astype(jnp.float32), width, axis=0)
    return jnp.repeat(grown, width, axis=1)


def product(a, b):
    return jnp.dot(a, b, precision=lax.Precision.HIGH, preferred_element_type=jnp.float32)


def sign(at):
    return 1 - 2 * ((at["x"] + at["c"]) % 2)


def body(amplitudes, integrals, pair_mask, tile_mask):
    l = lax.axis_index("l")
    width = amplitudes.shape[1] // pair_mask.shape[1]
    masked_v = integrals * expand(tile_mask, width)
    far_half = send(masked_v, ("l",), lambda at: {"l": at["l"] + 1})
    near = lax.all_gather(masked_v, "c", axis=1, tiled=True)
    near_beside = send(near, ("c", "x"), lambda at: {"x": at["x"] + sign(at)})
    masked_t = amplitudes * expand(pair_mask, width)
    names = ("h", "c", "x")
    own = jnp.concatenate([
        send(masked_t, names, lambda at: {"h": at["h"] - at["x"]}),
        send(masked_t, names, lambda at: {"h": at["h"] - at["x"] + sign(at)}),
    ])
    beside = jnp.concatenate([
        send(masked_t, names, lambda at: {"h": at["h"] - at["x"] - sign(at), "x": at["x"] + sign(at)}),
        send(masked_t, names, lambda at: {"h": at["h"] - at["x"] - 2 * sign(at), "x": at["x"] + sign(at)}),
    ])
    far = lax.all_gather(far_half, "c", axis=1, tiled=True)
    far_beside = send(far, ("c", "x"), lambda at: {"x": at["x"] + sign(at)})
    near_sum = product(own, near) + product(beside, near_beside)
    far_sum = product(own, far) + product(beside, far_beside)
    away = jnp.concatenate([near_sum[128:], far_sum[128:]], axis=1)
    came = send(away, ("c", "x"), lambda at: {"x": at["x"] - sign(at)})
    near_sum, far_sum = near_sum[:128] + came[:, :512], far_sum[:128] + came[:, 512:]
    low = l == 0
    halves = jnp.concatenate([jnp.where(low, near_sum, far_sum), jnp.where(low, far_sum, near_sum)], axis=1)
    pieces = halves.reshape(128, 8, 128).transpose(1, 0, 2)
    groups = []
    for first in range(0, 512, 8):
        core = first // 32 % 2
        groups.append([first + (k + 4 * core) % 8 for k in range(8)])
    turn = lax.axis_index("c") * 4
    pieces = jnp.concatenate([pieces, pieces[:4]])
    pieces = lax.dynamic_slice_in_dim(pieces, turn, 8, 0)
    total = lax.all_to_all(pieces, AXES, 0, 0, tiled=True, axis_index_groups=groups).sum(0)
    return send(total, ("h", "x"), lambda at: {"h": at["h"] + at["x"], "x": at["h"]})


def solution(mesh):
    fine = Mesh(mesh.devices.reshape(SIZES), AXES)
    occ, vir = ("h", "l", "c"), ("x", "z")
    in_specs = (P(occ, vir), P(vir, occ), P(occ, vir), P(vir, occ))
    return jax.shard_map(body, mesh=fine, in_specs=in_specs, out_specs=P(occ, vir), check_vma=False)
```

```python
import jax
import jax.numpy as jnp
from jax import lax
from jax.experimental import pallas as pl
from jax.experimental.pallas import tpu as pltpu
from jax.sharding import Mesh, PartitionSpec as P

AXES = ("h", "l", "c", "x", "z")
SIZES = (4, 2, 2, 4, 8)


def moves(names, target):
    sizes = [SIZES[AXES.index(name)] for name in names]
    pairs = []
    total = 1
    for size in sizes:
        total *= size
    for source in range(total):
        rest, at = source, {}
        for name, size in zip(names[::-1], sizes[::-1]):
            at[name], rest = rest % size, rest // size
        to = dict(at, **target(at))
        index = 0
        for name, size in zip(names, sizes):
            index = index * size + to[name] % size
        pairs.append((source, index))
    return pairs


def send(value, names, target):
    return lax.ppermute(value, names, moves(names, target))


def expand(mask, width):
    grown = jnp.repeat(mask.astype(jnp.float32), width, axis=0)
    return jnp.repeat(grown, width, axis=1)


def product(a, b):
    return jnp.dot(a, b, precision=lax.Precision.HIGH, preferred_element_type=jnp.float32)


def sign(at):
    return 1 - 2 * ((at["x"] + at["c"]) % 2)


def stage_rows(own, beside):
    def kernel(own_ref, beside_ref, out_ref):
        out_ref[:, :384], out_ref[:, 384:] = own_ref[...], beside_ref[...]

    vmem = pl.BlockSpec(memory_space=pltpu.VMEM)
    return pl.pallas_call(
        kernel,
        out_shape=jax.ShapeDtypeStruct((128, 768), jnp.float32),
        in_specs=[vmem] * 2,
        out_specs=vmem,
        cost_estimate=pl.CostEstimate(flops=10**10, bytes_accessed=1 << 20, transcendentals=0),
    )(own, beside)


def body(amplitudes, integrals, pair_mask, tile_mask):
    l = lax.axis_index("l")
    width = amplitudes.shape[1] // pair_mask.shape[1]
    masked_v = integrals * expand(tile_mask, width)
    far_half = send(masked_v, ("l",), lambda at: {"l": at["l"] + 1})
    near = lax.all_gather(masked_v, "c", axis=1, tiled=True)
    near_beside = send(near, ("c", "x"), lambda at: {"x": at["x"] + sign(at)})
    masked_t = amplitudes * expand(pair_mask, width)
    names = ("h", "c", "x")
    own_b = send(masked_t, names, lambda at: {"h": at["h"] - at["x"] + sign(at)})
    beside_b = send(masked_t, names, lambda at: {"h": at["h"] - at["x"] - 2 * sign(at), "x": at["x"] + sign(at)})
    staged = stage_rows(own_b, beside_b)
    own_b, beside_b = staged[:, :384], staged[:, 384:]
    far = lax.all_gather(far_half, "c", axis=1, tiled=True)
    masked_t, far = lax.optimization_barrier((masked_t, far))
    own_a = send(masked_t, names, lambda at: {"h": at["h"] - at["x"]})
    beside_a = send(masked_t, names, lambda at: {"h": at["h"] - at["x"] - sign(at), "x": at["x"] + sign(at)})
    far_beside = send(far, ("c", "x"), lambda at: {"x": at["x"] + sign(at)})
    def block(own, beside, near, near_beside, far, far_beside):
        near_block = product(own, near) + product(beside, near_beside)
        return jnp.concatenate([near_block, product(own, far) + product(beside, far_beside)], axis=1)

    integrals_held = (near, near_beside, far, far_beside)
    away = block(own_b, beside_b, *integrals_held)
    came = send(away, ("c", "x"), lambda at: {"x": at["x"] - sign(at)})
    *integrals_held, away = lax.optimization_barrier((*integrals_held, away))
    sums = block(own_a, beside_a, *integrals_held) + came
    near_sum, far_sum = sums[:, :512], sums[:, 512:]
    low = l == 0
    halves = jnp.concatenate([jnp.where(low, near_sum, far_sum), jnp.where(low, far_sum, near_sum)], axis=1)
    pieces = halves.reshape(128, 8, 128).transpose(1, 0, 2)
    groups = []
    for first in range(0, 512, 8):
        core = first // 32 % 2
        groups.append([first + (k + 4 * core) % 8 for k in range(8)])
    turn = lax.axis_index("c") * 4
    pieces = jnp.concatenate([pieces, pieces[:4]])
    pieces = lax.dynamic_slice_in_dim(pieces, turn, 8, 0)
    total = lax.all_to_all(pieces, AXES, 0, 0, tiled=True, axis_index_groups=groups).sum(0)
    return send(total, ("h", "x"), lambda at: {"h": at["h"] + at["x"], "x": at["h"]})


def solution(mesh):
    fine = Mesh(mesh.devices.reshape(SIZES), AXES)
    occ, vir = ("h", "l", "c"), ("x", "z")
    in_specs = (P(occ, vir), P(vir, occ), P(occ, vir), P(vir, occ))
    return jax.shard_map(body, mesh=fine, in_specs=in_specs, out_specs=P(occ, vir), check_vma=False)
```

```python
import jax
import jax.numpy as jnp
from jax import lax
from jax.experimental import pallas as pl
from jax.experimental.pallas import tpu as pltpu
from jax.sharding import Mesh, PartitionSpec as P

AXES = ("h", "l", "c", "x", "z")
SIZES = (4, 2, 2, 4, 8)


def moves(names, target):
    sizes = [SIZES[AXES.index(name)] for name in names]
    pairs = []
    total = 1
    for size in sizes:
        total *= size
    for source in range(total):
        rest, at = source, {}
        for name, size in zip(names[::-1], sizes[::-1]):
            at[name], rest = rest % size, rest // size
        to = dict(at, **target(at))
        index = 0
        for name, size in zip(names, sizes):
            index = index * size + to[name] % size
        pairs.append((source, index))
    return pairs


def send(value, names, target):
    return lax.ppermute(value, names, moves(names, target))


def expand(mask, width):
    grown = jnp.repeat(mask.astype(jnp.float32), width, axis=0)
    return jnp.repeat(grown, width, axis=1)


def product(a, b):
    return jnp.dot(a, b, precision=lax.Precision.HIGH, preferred_element_type=jnp.float32)


def sign(at):
    return 1 - 2 * ((at["x"] + at["c"]) % 2)


def stage_rows(own, beside):
    def kernel(own_ref, beside_ref, out_ref):
        out_ref[:, :384], out_ref[:, 384:] = own_ref[...], beside_ref[...]

    vmem = pl.BlockSpec(memory_space=pltpu.VMEM)
    return pl.pallas_call(
        kernel,
        out_shape=jax.ShapeDtypeStruct((128, 768), jnp.float32),
        in_specs=[vmem] * 2,
        out_specs=vmem,
        cost_estimate=pl.CostEstimate(flops=10**10, bytes_accessed=1 << 20, transcendentals=0),
    )(own, beside)


def ahead(at):
    return at["x"] + 2 * at["l"]


def body(amplitudes, integrals, pair_mask, tile_mask):
    l = lax.axis_index("l")
    width = amplitudes.shape[1] // pair_mask.shape[1]
    masked_v = integrals * expand(tile_mask, width)
    far_half = send(masked_v, ("l",), lambda at: {"l": at["l"] + 1})
    near = lax.all_gather(masked_v, "c", axis=1, tiled=True)
    near_beside = send(near, ("c", "x"), lambda at: {"x": at["x"] + sign(at)})
    masked_t = amplitudes * expand(pair_mask, width)
    names = ("h", "l", "c", "x")
    own_b = send(masked_t, names, lambda at: {"h": at["h"] - ahead(at) + sign(at)})
    beside_b = send(masked_t, names, lambda at: {"h": at["h"] - ahead(at) - 2 * sign(at), "x": at["x"] + sign(at)})
    staged = stage_rows(own_b, beside_b)
    own_b, beside_b = staged[:, :384], staged[:, 384:]
    far = lax.all_gather(far_half, "c", axis=1, tiled=True)
    masked_t, far = lax.optimization_barrier((masked_t, far))
    own_a = send(masked_t, names, lambda at: {"h": at["h"] - ahead(at)})
    beside_a = send(masked_t, names, lambda at: {"h": at["h"] - ahead(at) - sign(at), "x": at["x"] + sign(at)})
    far_beside = send(far, ("c", "x"), lambda at: {"x": at["x"] + sign(at)})
    def block(own, beside, near, near_beside, far, far_beside):
        near_block = product(own, near) + product(beside, near_beside)
        return jnp.concatenate([near_block, product(own, far) + product(beside, far_beside)], axis=1)

    integrals_held = (near, near_beside, far, far_beside)
    away = block(own_b, beside_b, *integrals_held)
    came = send(away, ("c", "x"), lambda at: {"x": at["x"] - sign(at)})
    *integrals_held, away = lax.optimization_barrier((*integrals_held, away))
    sums = block(own_a, beside_a, *integrals_held) + came
    near_sum, far_sum = sums[:, :512], sums[:, 512:]
    low = l == 0
    halves = jnp.concatenate([jnp.where(low, near_sum, far_sum), jnp.where(low, far_sum, near_sum)], axis=1)
    pieces = halves.reshape(128, 8, 128).transpose(1, 0, 2)
    groups = []
    for first in range(0, 512, 8):
        core = first // 32 % 2
        groups.append([first + (k + 4 * core) % 8 for k in range(8)])
    turn = lax.axis_index("c") * 4
    pieces = jnp.concatenate([pieces, pieces[:4]])
    pieces = lax.dynamic_slice_in_dim(pieces, turn, 8, 0)
    total = lax.all_to_all(pieces, AXES, 0, 0, tiled=True, axis_index_groups=groups).sum(0)
    return send(total, ("h", "l", "x"), lambda at: {"h": at["h"] + ahead(at), "x": at["h"]})


def solution(mesh):
    fine = Mesh(mesh.devices.reshape(SIZES), AXES)
    occ, vir = ("h", "l", "c"), ("x", "z")
    in_specs = (P(occ, vir), P(vir, occ), P(occ, vir), P(vir, occ))
    return jax.shard_map(body, mesh=fine, in_specs=in_specs, out_specs=P(occ, vir), check_vma=False)
```

```python
import jax
import jax.numpy as jnp
from jax import lax
from jax.experimental import pallas as pl
from jax.experimental.pallas import tpu as pltpu
from jax.sharding import Mesh, PartitionSpec as P

AXES = ("h", "l", "c", "x", "z")
SIZES = (4, 2, 2, 4, 8)


def moves(names, target):
    sizes = [SIZES[AXES.index(name)] for name in names]
    pairs = []
    total = 1
    for size in sizes:
        total *= size
    for source in range(total):
        rest, at = source, {}
        for name, size in zip(names[::-1], sizes[::-1]):
            at[name], rest = rest % size, rest // size
        to = dict(at, **target(at))
        index = 0
        for name, size in zip(names, sizes):
            index = index * size + to[name] % size
        pairs.append((source, index))
    return pairs


def send(value, names, target):
    return lax.ppermute(value, names, moves(names, target))


def expand(mask, width):
    grown = jnp.repeat(mask.astype(jnp.float32), width, axis=0)
    return jnp.repeat(grown, width, axis=1)


def product(a, b):
    return jnp.dot(a, b, precision=lax.Precision.HIGH, preferred_element_type=jnp.float32)


def sign(at):
    return 1 - 2 * ((at["x"] + at["c"]) % 2)


def stage_rows(own, beside):
    def kernel(own_ref, beside_ref, out_ref):
        out_ref[:, :384], out_ref[:, 384:] = own_ref[...], beside_ref[...]

    vmem = pl.BlockSpec(memory_space=pltpu.VMEM)
    return pl.pallas_call(
        kernel,
        out_shape=jax.ShapeDtypeStruct((128, 768), jnp.float32),
        in_specs=[vmem] * 2,
        out_specs=vmem,
        cost_estimate=pl.CostEstimate(flops=10**10, bytes_accessed=1 << 20, transcendentals=0),
    )(own, beside)


def ahead(at):
    return at["x"] + 2 * at["l"] + 1


def body(amplitudes, integrals, pair_mask, tile_mask):
    l = lax.axis_index("l")
    width = amplitudes.shape[1] // pair_mask.shape[1]
    masked_v = integrals * expand(tile_mask, width)
    far_half = send(masked_v, ("l",), lambda at: {"l": at["l"] + 1})
    near = lax.all_gather(masked_v, "c", axis=1, tiled=True)
    near_beside = send(near, ("c", "x"), lambda at: {"x": at["x"] + sign(at)})
    masked_t = amplitudes * expand(pair_mask, width)
    names = ("h", "l", "c", "x")
    own_b = send(masked_t, names, lambda at: {"h": at["h"] - ahead(at) + sign(at)})
    beside_b = send(masked_t, names, lambda at: {"h": at["h"] - ahead(at) - 2 * sign(at), "x": at["x"] + sign(at)})
    staged = stage_rows(own_b, beside_b)
    own_b, beside_b = staged[:, :384], staged[:, 384:]
    far = lax.all_gather(far_half, "c", axis=1, tiled=True)
    masked_t, far = lax.optimization_barrier((masked_t, far))
    own_a = send(masked_t, names, lambda at: {"h": at["h"] - ahead(at)})
    beside_a = send(masked_t, names, lambda at: {"h": at["h"] - ahead(at) - sign(at), "x": at["x"] + sign(at)})
    far_beside = send(far, ("c", "x"), lambda at: {"x": at["x"] + sign(at)})
    def block(own, beside, near, near_beside, far, far_beside):
        near_block = product(own, near) + product(beside, near_beside)
        return jnp.concatenate([near_block, product(own, far) + product(beside, far_beside)], axis=1)

    integrals_held = (near, near_beside, far, far_beside)
    away = block(own_b, beside_b, *integrals_held)
    came = send(away, ("c", "x"), lambda at: {"x": at["x"] - sign(at)})
    *integrals_held, away = lax.optimization_barrier((*integrals_held, away))
    sums = block(own_a, beside_a, *integrals_held) + came
    near_sum, far_sum = sums[:, :512], sums[:, 512:]
    low = l == 0
    halves = jnp.concatenate([jnp.where(low, near_sum, far_sum), jnp.where(low, far_sum, near_sum)], axis=1)
    pieces = halves.reshape(128, 8, 128).transpose(1, 0, 2)
    groups = []
    for first in range(0, 512, 8):
        core = first // 32 % 2
        groups.append([first + (k + 4 * core) % 8 for k in range(8)])
    turn = lax.axis_index("c") * 4
    pieces = jnp.concatenate([pieces, pieces[:4]])
    pieces = lax.dynamic_slice_in_dim(pieces, turn, 8, 0)
    total = lax.all_to_all(pieces, AXES, 0, 0, tiled=True, axis_index_groups=groups).sum(0)
    return send(total, ("h", "l", "x"), lambda at: {"h": at["h"] + ahead(at), "x": at["h"]})


def solution(mesh):
    fine = Mesh(mesh.devices.reshape(SIZES), AXES)
    occ, vir = ("h", "l", "c"), ("x", "z")
    in_specs = (P(occ, vir), P(vir, occ), P(occ, vir), P(vir, occ))
    return jax.shard_map(body, mesh=fine, in_specs=in_specs, out_specs=P(occ, vir), check_vma=False)
```
